256 devices in a mesh: site: 16 (over x, y), sector: 16 (over z, core).
Axes of the slice: x: 4, y: 4, z: 8, core: 2. Of those that a mesh axis runs over, the one named last changes fastest.
Arguments:
- boundary: bfloat16 [16, 4096, 32, 256], P('site', 'sector'), may hold values from -0.375 to 0.375
- peps_row: bfloat16 [16, 32, 8], P('site'), may hold values from -1 to 1
- sketch: bfloat16 [16, 4096, 8, 256], P('site', 'sector'), may hold values from -0.125 to 0.125
- charges: int32 [16, 8], P('site'), may hold values from -1 to 1
- left_edge: bfloat16 [512, 4096], P(None, 'sector'), may hold values from -6 to 6
Outputs:
- environments: float32 [16, 512, 4096], P('site', None, 'sector')
The draws below stay inside these ranges and needn't reach their ends.
Inputs may be any that keep to these rules, and one draw needn't show every extreme that they name: `charges`: each entry is a charge change of -1, 0 or +1.
All inputs are finite; a program needn't handle non-finite values.
Results may differ from the reference program's by a relative error of at most 0.0003.
Values sent between devices are 32-bit elements; how exact they have to be, the bound alone decides.
No kernel may reach another device: no remote copies, remote signals or barrier semaphores. Data moves between devices by JAX's collectives and lax.ppermute only.
A program may use at most 64 MiB of HBM per device.

```python
import jax
import jax.numpy as jnp
from jax import lax

W = 256
P_SIZE = 32
D = 8
ROWS = 512
SITES = 16
CHI = 4096
N_SECTOR = 16


def place_ends(values, own_key, least, high):
    shape = values.shape
    spot = [jax.random.randint(jax.random.fold_in(own_key, axis), (), 0, shape[axis]) for axis in range(len(shape))]
    values = values.at[tuple(spot)].set(least)
    longest = shape.index(max(shape))
    spot[longest] = (spot[longest] + 1) % shape[longest]
    return values.at[tuple(spot)].set(high)


def level_of(stream_key, extent, pieces, low, top_value):
    level, own = 1.0, jax.random.fold_in(stream_key, 6)
    for axis_at, blocks in pieces:
        heights = jnp.exp(jax.random.uniform(jax.random.fold_in(own, axis_at), (blocks,), jnp.float32, low / len(pieces), top_value / len(pieces)))
        level = level * jnp.repeat(heights, extent[axis_at] // blocks).reshape([-1 if axis == axis_at else 1 for axis in range(len(extent))])
    return level


def centred(own_key, extent, scale, bound, split=(), held_as=jnp.bfloat16):
    level = level_of(own_key, extent, split, -0.22, 0.18) if split else 1.0
    entries = jax.random.normal(own_key, extent, jnp.float32) * scale * level
    return jnp.minimum(jnp.maximum(entries, -bound), bound).astype(held_as)


def setup_inputs(seed: int = 0) -> dict:
    key_of = jax.random.split(jax.random.key(seed), 6)
    return {
        "boundary": centred(key_of[0], (SITES, CHI, P_SIZE, W), W ** -0.5, 0.375, ((0, 16), (1, 16))),
        "peps_row": centred(key_of[1], (SITES, P_SIZE, D), P_SIZE ** -0.5, 1.0, ((0, 16),)),
        "sketch": centred(key_of[2], (SITES, CHI, D, W), (W * D) ** -0.5, 0.125, ((0, 16), (1, 16))),
        "charges": place_ends(jax.random.randint(key_of[3], (SITES, D), -1, 2), jax.random.fold_in(key_of[3], 1), -1, 1).astype(jnp.int32),
        "left_edge": centred(key_of[4], (ROWS, CHI), 1.0, 6.0, ((1, 16),)),
    }


def reference(boundary, peps_row, sketch, charges, left_edge):
    absorbed = jnp.einsum('jipv,jpl->jilv', boundary.astype(jnp.float32), peps_row.astype(jnp.float32), precision=lax.Precision.HIGHEST)

    def absorb_site(state_rows, inputs):
        block_tensor, block_sketch, charge_row = inputs
        block_tensor = block_tensor.reshape(N_SECTOR, W, D, W)
        block_sketch = block_sketch.astype(jnp.float32).reshape(N_SECTOR, W, D, W)
        onehot = (charge_row[:, None] == jnp.arange(-1, 2, dtype=jnp.int32)[None, :]).astype(jnp.float32)
        transfer = jnp.einsum('bwlv,bvlu,ls->bswu', block_tensor, block_sketch, onehot, precision=lax.Precision.HIGHEST)
        blocked = state_rows.reshape(ROWS, N_SECTOR, W)
        parts = jnp.einsum('rbw,bswu->srbu', blocked, transfer, precision=lax.Precision.HIGHEST)
        empty_rows = jnp.zeros((ROWS, 1, W), jnp.float32)
        updated = parts[1] + jnp.concatenate([empty_rows, parts[2][:, :-1]], axis=1) + jnp.concatenate([parts[0][:, 1:], empty_rows], axis=1)
        updated = updated.reshape(ROWS, N_SECTOR * W)
        return updated, updated

    start_rows = left_edge.astype(jnp.float32)
    final_rows, environments = lax.scan(absorb_site, start_rows, (absorbed, sketch, charges))
    return environments
```

```python
import functools

import jax
import jax.numpy as jnp
from jax import lax
from jax.experimental import pallas as pl
from jax.experimental.pallas import tpu as pltpu
from jax.sharding import PartitionSpec as P

GROUP = 4
CHARGES = 3
LANES = 128


def dot(a, b):
    return jnp.dot(a, b, preferred_element_type=jnp.float32)


def split(x):
    high = x.astype(jnp.bfloat16)
    return high, (x - high.astype(jnp.float32)).astype(jnp.bfloat16)


def transfer_kernel(charge_ref, sign_ref, peps_ref, boundary_ref, sketch_ref,
                    top_ref, bottom_ref, spread, absorbed, wide, total):
    width = total.shape[1]
    phys, bonds = peps_ref.shape
    per = width // phys
    step = pl.program_id(0)
    chunks = boundary_ref.shape[0] // width

    @pl.when(step == 0)
    def _():
        for lane in range(width // LANES):
            wide[lane] = sketch_ref[:, lane * LANES:(lane + 1) * LANES].astype(jnp.float32)
        row = lax.broadcasted_iota(jnp.int32, (phys, width), 0)
        col = lax.broadcasted_iota(jnp.int32, (phys, width), 1)
        tiled = jnp.where(lax.rem(col, phys) == row, 1.0, 0.0).astype(jnp.bfloat16)
        repeated = lax.dot_general(
            peps_ref[...], tiled, (((0,), (0,)), ((), ())), preferred_element_type=jnp.float32
        )
        rows = bonds * per
        pick_row = lax.broadcasted_iota(jnp.int32, (rows, bonds), 0)
        pick_col = lax.broadcasted_iota(jnp.int32, (rows, bonds), 1)
        pick = jnp.where(lax.div(pick_row, per) == pick_col, 1.0, 0.0).astype(jnp.bfloat16)
        spread_rows = dot(pick, repeated.astype(jnp.bfloat16))
        out_row = lax.broadcasted_iota(jnp.int32, (rows, width), 0)
        out_col = lax.broadcasted_iota(jnp.int32, (rows, width), 1)
        keep = lax.rem(out_row, per) == lax.div(out_col, phys)
        spread[...] = jnp.where(keep, spread_rows, 0.0).astype(jnp.bfloat16)

    for chunk in range(chunks):
        piece = dot(spread[...], boundary_ref[chunk * width:(chunk + 1) * width, :])
        at = (step * chunks + chunk) * per
        for bond in range(bonds):
            absorbed[bond, pl.ds(pl.multiple_of(at, per), per), :] = piece[bond * per:(bond + 1) * per]

    @pl.when(step == pl.num_programs(0) - 1)
    def _():
        total[...] = jnp.zeros_like(total)
        for bond in range(bonds):
            high, low = split(absorbed[bond])
            lanes = [wide[lane, pl.ds(bond, width, stride=bonds), :] for lane in range(width // LANES)]
            part = jnp.concatenate(lanes, axis=1).astype(jnp.bfloat16)
            both = dot(jnp.concatenate([high, low], axis=0), part)
            slot = 1 + charge_ref[bond] * sign_ref[0]
            where = pl.ds(pl.multiple_of(slot * width, width), width)
            total[where, :] += both[:width] + both[width:]
        half = total.shape[0] // 2
        top_ref[...] = total[:half]
        bottom_ref[...] = total[half:]


def transfer(boundary, peps_row, sketch, charges, sign):
    width = boundary.shape[3]
    phys, bonds = peps_row.shape[1:]
    flat = boundary.reshape(width * phys, width)
    steps = 8
    half = jax.ShapeDtypeStruct((CHARGES * width // 2, width), jnp.float32)
    whole = lambda shape: pl.BlockSpec(shape, lambda i: (0,) * len(shape))
    return pl.pallas_call(
        transfer_kernel,
        grid=(steps,),
        out_shape=(half, half),
        in_specs=[
            pl.BlockSpec(memory_space=pltpu.SMEM),
            pl.BlockSpec(memory_space=pltpu.SMEM),
            whole((phys, bonds)),
            pl.BlockSpec((width * phys // steps, width), lambda i: (i, 0)),
            whole((width * bonds, width)),
        ],
        out_specs=(whole(half.shape), whole(half.shape)),
        scratch_shapes=[
            pltpu.VMEM((bonds * width // phys, width), jnp.bfloat16),
            pltpu.VMEM((bonds, width, width), jnp.float32),
            pltpu.VMEM((width // LANES, width * bonds, LANES), jnp.float32),
            pltpu.VMEM((CHARGES * width, width), jnp.float32),
        ],
        compiler_params=pltpu.CompilerParams(vmem_limit_bytes=32 * 2**20),
        name="transfer",
    )(charges[0], sign, peps_row[0], flat, sketch.reshape(width * bonds, width))


def load_transfer(which_ref, pieces, high_ref, low_ref, buffer, sem):
    half = buffer.shape[0] // 2
    for k in range(GROUP):
        @pl.when(which_ref[0] == k)
        def _():
            pltpu.make_async_copy(pieces[2 * k], buffer.at[pl.ds(0, half)], sem).start()
            pltpu.make_async_copy(pieces[2 * k + 1], buffer.at[pl.ds(half, half)], sem).start()
    pltpu.make_async_copy(buffer, buffer, sem).wait()
    high, low = split(buffer[...])
    high_ref[...] = high
    low_ref[...] = low


def prepare_kernel(which_ref, *refs):
    load_transfer(which_ref, refs[:8], *refs[8:])


def times(state, high, low):
    rows = state.shape[0]
    state_high, state_low = split(state)
    first = dot(jnp.concatenate([state_high, state_low], axis=0), high)
    return first[:rows] + first[rows:] + dot(state_high, low)


VMEM = pl.BlockSpec(memory_space=pltpu.VMEM)
SMEM = pl.BlockSpec(memory_space=pltpu.SMEM)
ANY = pl.BlockSpec(memory_space=pl.ANY)


def prepare(which, pieces):
    rows, width = pieces[0].shape
    out = jax.ShapeDtypeStruct((2 * rows, width), jnp.bfloat16)
    return pl.pallas_call(
        prepare_kernel,
        out_shape=(out, out),
        in_specs=[SMEM] + [ANY] * 8,
        out_specs=(VMEM, VMEM),
        scratch_shapes=[pltpu.VMEM((2 * rows, width), jnp.float32), pltpu.SemaphoreType.DMA],
        cost_estimate=pl.CostEstimate(flops=0, bytes_accessed=12 * rows * width * 2, transcendentals=0),
        name="prepare",
    )(which, *pieces)


def away_of(state, high_ref, low_ref, out_a, out_b):
    width = state.shape[1]
    out_b[...] = times(state, high_ref[:width], low_ref[:width])
    out_a[...] = times(state, high_ref[2 * width:], low_ref[2 * width:])


def away_kernel(state_ref, high_ref, low_ref, out_a, out_b):
    away_of(state_ref[...], high_ref, low_ref, out_a, out_b)


def summed(edge_ref, stay_ref, from_a, from_b):
    keep = edge_ref[0] == 0
    return stay_ref[...] + from_a[...] + jnp.where(keep, from_b[...], 0.0)


def sum_away_kernel(edge_ref, stay_ref, from_a, from_b, high_ref, low_ref, state_ref, out_a, out_b):
    state = summed(edge_ref, stay_ref, from_a, from_b)
    state_ref[...] = state
    away_of(state, high_ref, low_ref, out_a, out_b)


def sum_kernel(edge_ref, stay_ref, from_a, from_b, state_ref):
    state_ref[...] = summed(edge_ref, stay_ref, from_a, from_b)


def stay_kernel(state_ref, high_ref, low_ref, out_ref):
    width = state_ref.shape[1]
    out_ref[...] = times(state_ref[...], high_ref[width:2 * width], low_ref[width:2 * width])


def call(kernel, outs, smem, arrays, tiles, name):
    shape = jax.ShapeDtypeStruct(arrays[0].shape, jnp.float32)
    rows, width = shape.shape
    flops = 2 * 3 * tiles * rows * width * width
    moved = sum(a.size * a.dtype.itemsize for a in arrays) + 4 * outs * rows * width
    return pl.pallas_call(
        kernel,
        out_shape=(shape,) * outs if outs > 1 else shape,
        in_specs=[SMEM] * len(smem) + [VMEM] * len(arrays),
        out_specs=(VMEM,) * outs if outs > 1 else VMEM,
        cost_estimate=pl.CostEstimate(flops=flops, bytes_accessed=moved, transcendentals=0),
        name=name,
    )(*smem, *arrays)


def local(boundary, peps_row, sketch, charges, left_edge):
    sites = lax.axis_size("site")
    sectors = lax.axis_size("sector")
    position = lax.axis_index("site")
    block = lax.axis_index("sector")
    x, y = position // GROUP, lax.rem(position, GROUP)
    rows, width = left_edge.shape
    slab = rows // GROUP

    inside = [(i, i ^ 1) for i in range(sectors)]
    across = [(i, (i - 1) % sectors if i % 2 == 0 else (i + 1) % sectors) for i in range(sectors)]
    ring = lambda by: [(i, i - i % GROUP + (i + by) % GROUP) for i in range(sites)]
    hop = [(i, (i + GROUP) % sites) for i in range(sites)]

    odd = lax.rem(block, 2)
    sign = jnp.full((1,), 1, jnp.int32) - 2 * odd
    edge = jnp.logical_or(block == 0, block == sectors - 1).astype(jnp.int32).reshape(1)

    top, bottom = transfer(boundary, peps_row, sketch, charges, sign)
    up_top = lax.ppermute(top, "site", ring(-1))
    down_bottom = lax.ppermute(bottom, "site", ring(1))
    up_bottom = lax.ppermute(bottom, "site", ring(-1))
    down_top = lax.ppermute(top, "site", ring(1))
    far_top = lax.ppermute(up_top, "site", ring(-1))
    far_bottom = lax.ppermute(down_bottom, "site", ring(1))
    pieces = (top, bottom, up_top, up_bottom, far_top, far_bottom, down_top, down_bottom)

    state = lax.dynamic_slice_in_dim(left_edge, y * slab, slab, 0).astype(jnp.float32)
    transfers = [
        prepare(lax.rem(GROUP + j - y, GROUP).reshape(1), pieces) for j in range(GROUP)
    ]

    kept = [None] * GROUP
    for phase in range(sites // GROUP):
        out_a, out_b = call(away_kernel, 2, (), (state, *transfers[0]), 2, "away")
        for j in range(GROUP):
            from_b = lax.ppermute(out_b, "sector", across)
            from_a = lax.ppermute(out_a, "sector", inside)
            stay = call(stay_kernel, 1, (), (state, *transfers[j]), 1, "stay")
            if j < GROUP - 1:
                state, out_a, out_b = call(
                    sum_away_kernel, 3, (edge,), (stay, from_a, from_b, *transfers[j + 1]), 2, "sum_away"
                )
            else:
                state = call(sum_kernel, 1, (edge,), (stay, from_a, from_b), 0, "sum")
            kept[j] = state if phase == 0 else jnp.where(x == phase, state, kept[j])
        if phase < sites // GROUP - 1:
            state = lax.ppermute(state, "site", hop)

    stacked = jnp.stack(kept)
    result = jnp.zeros((1, rows, width), jnp.float32)
    for by in range(GROUP):
        out = lax.dynamic_index_in_dim(stacked, lax.rem(y + by, GROUP), 0, keepdims=True)
        if by:
            out = lax.ppermute(out, "site", ring(by))
        at = lax.rem(GROUP + y - by, GROUP) * slab
        result = lax.dynamic_update_slice(result, out, (0, at, 0))
    return result


def solution(mesh):
    in_specs = (
        P("site", "sector", None, None),
        P("site", None, None),
        P("site", "sector", None, None),
        P("site", None),
        P(None, "sector"),
    )
    out_specs = P("site", None, "sector")
    return jax.shard_map(local, mesh=mesh, in_specs=in_specs, out_specs=out_specs, check_vma=False)
```

```python
import functools

import jax
import jax.numpy as jnp
from jax import lax
from jax.experimental import pallas as pl
from jax.experimental.pallas import tpu as pltpu
from jax.sharding import PartitionSpec as P

GROUP = 4
CHARGES = 3
LANES = 128
SMALL = 12 * 2**20
LARGE = 56 * 2**20


def dot(a, b):
    return jnp.dot(a, b, preferred_element_type=jnp.float32)


def split(x):
    high = x.astype(jnp.bfloat16)
    return high, (x - high.astype(jnp.float32)).astype(jnp.bfloat16)


def transfer_kernel(x_ref, y_ref, sign_ref, inner_ref, charge_ref, peps_ref, boundary_ref, sketch_ref, top_ref, bottom_ref,
                    boundary, sketch, spread, absorbed, wide, total, sems):
    width = total.shape[1]
    bonds, phys = peps_ref.shape
    per = width // phys
    parts = sems.shape[0] - 1
    span = boundary.shape[0] // parts
    chunks = span // width

    def fetch(part):
        rows = pl.ds(part * span, span)
        return pltpu.make_async_copy(boundary_ref.at[rows], boundary.at[rows], sems.at[part])

    fetch_sketch = pltpu.make_async_copy(sketch_ref, sketch, sems.at[parts])
    for part in range(parts):
        fetch(part).start()
    fetch_sketch.start()

    row = lax.broadcasted_iota(jnp.int32, (phys, width), 0)
    col = lax.broadcasted_iota(jnp.int32, (phys, width), 1)
    tiled = jnp.where(lax.rem(col, phys) == row, 1.0, 0.0).astype(jnp.bfloat16)
    repeated = lax.dot_general(
        peps_ref[...], tiled, (((1,), (0,)), ((), ())), preferred_element_type=jnp.float32
    )
    rows = bonds * per
    pick_row = lax.broadcasted_iota(jnp.int32, (rows, bonds), 0)
    pick_col = lax.broadcasted_iota(jnp.int32, (rows, bonds), 1)
    pick = jnp.where(lax.div(pick_row, per) == pick_col, 1.0, 0.0).astype(jnp.bfloat16)
    spread_rows = dot(pick, repeated.astype(jnp.bfloat16))
    out_row = lax.broadcasted_iota(jnp.int32, (rows, width), 0)
    out_col = lax.broadcasted_iota(jnp.int32, (rows, width), 1)
    keep = lax.rem(out_row, per) == lax.div(out_col, phys)
    spread[...] = jnp.where(keep, spread_rows, 0.0).astype(jnp.bfloat16)

    for part in range(parts):
        fetch(part).wait()
        for chunk in range(part * chunks, (part + 1) * chunks):
            piece = dot(spread[...], boundary[chunk * width:(chunk + 1) * width, :])
            for bond in range(bonds):
                absorbed[bond, chunk * per:(chunk + 1) * per, :] = piece[bond * per:(bond + 1) * per]

    fetch_sketch.wait()
    for lane in range(width // LANES):
        wide[lane] = sketch[:, lane * LANES:(lane + 1) * LANES].astype(jnp.float32)
    total[...] = jnp.zeros_like(total)
    for bond in range(bonds):
        high, low = split(absorbed[bond])
        lanes = [wide[lane, pl.ds(bond, width, stride=bonds), :] for lane in range(width // LANES)]
        part = jnp.concatenate(lanes, axis=1).astype(jnp.bfloat16)
        both = dot(jnp.concatenate([high, low], axis=0), part)
        slot = 1 + charge_ref[bond] * sign_ref[0]
        where = pl.ds(pl.multiple_of(slot * width, width), width)
        total[where, :] += both[:width] + both[width:]
    half = total.shape[0] // 2
    top_ref[...] = total[:half]
    bottom_ref[...] = total[half:]


VMEM = pl.BlockSpec(memory_space=pltpu.VMEM)
SMEM = pl.BlockSpec(memory_space=pltpu.SMEM)
ANY = pl.BlockSpec(memory_space=pl.ANY)


def transfer(info, boundary, peps_row, sketch, charges):
    width = boundary.shape[3]
    phys, bonds = peps_row.shape[1:]
    parts = 8
    half = jax.ShapeDtypeStruct((CHARGES * width // 2, width), jnp.float32)
    return pl.pallas_call(
        transfer_kernel,
        out_shape=(half, half),
        in_specs=[SMEM] * 5 + [VMEM, ANY, ANY],
        out_specs=(VMEM, VMEM),
        scratch_shapes=[
            pltpu.VMEM((width * phys, width), jnp.bfloat16),
            pltpu.VMEM((width * bonds, width), jnp.bfloat16),
            pltpu.VMEM((bonds * width // phys, width), jnp.bfloat16),
            pltpu.VMEM((bonds, width, width), jnp.float32),
            pltpu.VMEM((width // LANES, width * bonds, LANES), jnp.float32),
            pltpu.VMEM((CHARGES * width, width), jnp.float32),
            pltpu.SemaphoreType.DMA((parts + 1,)),
        ],
        compiler_params=pltpu.CompilerParams(vmem_limit_bytes=LARGE),
        name="transfer",
    )(*info, charges[0], peps_row[0].T, boundary.reshape(width * phys, width), sketch.reshape(width * bonds, width))


def times(state, high, low):
    rows = state.shape[0]
    state_high, state_low = split(state)
    first = dot(jnp.concatenate([state_high, state_low], axis=0), high)
    return first[:rows] + first[rows:] + dot(state_high, low)


def call(kernel, outs, scalars, arrays, tiles=0, aliases={}, name=None):
    moved = sum(a.size * a.dtype.itemsize for a in arrays)
    rows, width = 128, 256
    shapes = tuple(jax.ShapeDtypeStruct(*out) for out in outs)
    return pl.pallas_call(
        kernel,
        out_shape=shapes,
        in_specs=[SMEM] * len(scalars) + [VMEM] * len(arrays),
        out_specs=(VMEM,) * len(outs),
        input_output_aliases=aliases,
        cost_estimate=pl.CostEstimate(
            flops=6 * tiles * rows * width * width, bytes_accessed=moved, transcendentals=0
        ),
        compiler_params=pltpu.CompilerParams(vmem_limit_bytes=SMALL),
        name=name,
    )(*scalars, *arrays)


def place_kernel(k, y_ref, top_ref, bottom_ref, *refs):
    high_ref, low_ref = refs[-2:]
    half = top_ref.shape[0]
    at = lax.rem(y_ref[0] + k, GROUP) * (2 * half)
    for ref, offset in ((top_ref, 0), (bottom_ref, half)):
        where = pl.ds(pl.multiple_of(at + offset, half), half)
        high, low = split(ref[...])
        high_ref[where, :] = high
        low_ref[where, :] = low


def place(info, k, top, bottom, placed):
    half, width = top.shape
    out = ((GROUP * 2 * half, width), jnp.bfloat16)
    aliases = {3: 0, 4: 1} if placed else {}
    return call(
        functools.partial(place_kernel, k), (out, out), (info[Y],), (top, bottom, *placed), 0, aliases, "place"
    )


def columns(site, slot, width):
    start = (site * CHARGES + slot) * width
    return slice(start, start + width)


def away_of(site, state, high_ref, low_ref, out_a, out_b):
    width = state.shape[1]
    for slot, out in ((0, out_b), (2, out_a)):
        where = columns(site, slot, width)
        out[...] = times(state, high_ref[where], low_ref[where])


def edge_kernel(y_ref, edge_ref, high_ref, low_ref, state_ref, out_a, out_b):
    slab = state_ref.shape[0]
    at = pl.multiple_of(y_ref[0] * slab, slab)
    state = edge_ref[pl.ds(at, slab), :].astype(jnp.float32)
    state_ref[...] = state
    away_of(0, state, high_ref, low_ref, out_a, out_b)


def away_kernel(state_ref, high_ref, low_ref, out_a, out_b):
    away_of(0, state_ref[...], high_ref, low_ref, out_a, out_b)


def summed(inner_ref, stay_ref, from_a, from_b):
    return stay_ref[...] + from_a[...] + jnp.where(inner_ref[0] == 1, from_b[...], 0.0)


def sum_away_kernel(site, inner_ref, stay_ref, from_a, from_b, high_ref, low_ref, state_ref, out_a, out_b):
    state = summed(inner_ref, stay_ref, from_a, from_b)
    state_ref[...] = state
    away_of(site, state, high_ref, low_ref, out_a, out_b)


def keep_at(phase, site, x_ref, state, kept_ref):
    @pl.when(x_ref[0] == phase)
    def _():
        kept_ref[site] = state


def stay_kernel(phase, site, x_ref, state_ref, high_ref, low_ref, *refs):
    where = columns(site, 1, state_ref.shape[1])
    state = state_ref[...]
    if site:
        keep_at(phase, site - 1, x_ref, state, refs[-1])
        out_ref = refs[-2]
    else:
        out_ref = refs[-1]
    out_ref[...] = times(state, high_ref[where], low_ref[where])


def sum_kernel(phase, x_ref, inner_ref, stay_ref, from_a, from_b, old_ref, state_ref, kept_ref):
    state = summed(inner_ref, stay_ref, from_a, from_b)
    state_ref[...] = state
    keep_at(phase, GROUP - 1, x_ref, state, kept_ref)


def pick_kernel(y_ref, kept_ref, *outs):
    for by, out in enumerate(outs):
        out[...] = kept_ref[lax.rem(y_ref[0] + by + 1, GROUP)]


def lay_kernel(y_ref, kept_ref, *refs):
    out_ref = refs[-1]
    slab = kept_ref.shape[1]
    for by in range(GROUP):
        source = lax.rem(y_ref[0] + GROUP - by, GROUP)
        where = pl.ds(pl.multiple_of(source * slab, slab), slab)
        out_ref[0, where, :] = refs[by - 1][...] if by else kept_ref[y_ref[0]]


X, Y, SIGN, INNER = range(4)


def local(boundary, peps_row, sketch, charges, left_edge):
    sites = lax.axis_size("site")
    sectors = lax.axis_size("sector")
    position = lax.axis_index("site")
    block = lax.axis_index("sector")
    rows, width = left_edge.shape
    slab = rows // GROUP
    state_shape = ((slab, width), jnp.float32)
    kept_shape = ((GROUP, slab, width), jnp.float32)

    inside = [(i, i ^ 1) for i in range(sectors)]
    across = [(i, (i - 1) % sectors if i % 2 == 0 else (i + 1) % sectors) for i in range(sectors)]
    ring = lambda by: [(i, i - i % GROUP + (i + by) % GROUP) for i in range(sites)]
    hop = [(i, (i + GROUP) % sites) for i in range(sites)]

    inner = jnp.logical_and(block > 0, block < sectors - 1).astype(jnp.int32)
    info = [lax.div(position, GROUP), lax.rem(position, GROUP), 1 - 2 * lax.rem(block, 2), inner]
    info = lax.optimization_barrier([scalar.astype(jnp.int32).reshape(1) for scalar in info])

    top, bottom = transfer(info, boundary, peps_row, sketch, charges)
    up_top = lax.ppermute(top, "site", ring(-1))
    down_bottom = lax.ppermute(bottom, "site", ring(1))
    up_bottom = lax.ppermute(bottom, "site", ring(-1))
    down_top = lax.ppermute(top, "site", ring(1))
    far_top = lax.ppermute(up_top, "site", ring(-1))
    far_bottom = lax.ppermute(down_bottom, "site", ring(1))
    placed = place(info, 0, top, bottom, ())
    placed = place(info, 1, up_top, up_bottom, placed)
    placed = place(info, 3, down_top, down_bottom, placed)
    placed = place(info, 2, far_top, far_bottom, placed)

    state, out_a, out_b = call(
        edge_kernel, (state_shape,) * 3, (info[Y],), (left_edge, *placed), 2, name="away"
    )
    kept = None
    for phase in range(sites // GROUP):
        if phase:
            state = lax.ppermute(state, "site", hop)
            out_a, out_b = call(away_kernel, (state_shape,) * 2, (), (state, *placed), 2, name="away")
        for site in range(GROUP):
            from_b = lax.ppermute(out_b, "sector", across)
            from_a = lax.ppermute(out_a, "sector", inside)
            kernel = functools.partial(stay_kernel, phase, site)
            arrays = (state, *placed)
            if not site:
                stay, = call(kernel, (state_shape,), (info[X],), arrays, 1, name="stay")
            elif kept is None:
                stay, kept = call(kernel, (state_shape, kept_shape), (info[X],), arrays, 1, name="stay")
            else:
                stay, kept = call(kernel, (state_shape, kept_shape), (info[X],), (*arrays, kept), 1, {4: 1}, "stay")
            if site < GROUP - 1:
                kernel = functools.partial(sum_away_kernel, site + 1)
                arrays = (stay, from_a, from_b, *placed)
                state, out_a, out_b = call(kernel, (state_shape,) * 3, (info[INNER],), arrays, 2, name="sum_away")
            else:
                kernel = functools.partial(sum_kernel, phase)
                arrays = (stay, from_a, from_b, kept)
                scalars = (info[X], info[INNER])
                state, kept = call(kernel, (state_shape, kept_shape), scalars, arrays, 0, {5: 1}, "sum")

    sent = call(pick_kernel, (state_shape,) * (GROUP - 1), (info[Y],), (kept,), name="pick")
    came = [lax.ppermute(out, "site", ring(by + 1)) for by, out in enumerate(sent)]
    result, = call(lay_kernel, (((1, rows, width), jnp.float32),), (info[Y],), (kept, *came), name="lay")
    return result


def solution(mesh):
    in_specs = (
        P("site", "sector", None, None),
        P("site", None, None),
        P("site", "sector", None, None),
        P("site", None),
        P(None, "sector"),
    )
    out_specs = P("site", None, "sector")
    return jax.shard_map(local, mesh=mesh, in_specs=in_specs, out_specs=out_specs, check_vma=False)
```

```python
import functools

import jax
import jax.numpy as jnp
from jax import lax
from jax.experimental import pallas as pl
from jax.experimental.pallas import tpu as pltpu
from jax.sharding import PartitionSpec as P

GROUP = 4
CHARGES = 3
LANES = 128
SMALL = 12 * 2**20
WINDOW = 120
LARGE = 60 * 2**20


def dot(a, b):
    return jnp.dot(a, b, preferred_element_type=jnp.float32)


def split(x):
    high = x.astype(jnp.bfloat16)
    return high, (x - high.astype(jnp.float32)).astype(jnp.bfloat16)


def transfer_kernel(sign_ref, charge_ref, peps_ref, boundary_ref, sketch_ref, top_ref, bottom_ref,
                    boundary, sketch, spread, absorbed, wide, total, sems):
    width = total.shape[1]
    bonds, phys = peps_ref.shape
    per = width // phys
    parts = sems.shape[0] - 1
    span = boundary.shape[0] // parts
    chunks = span // width

    def fetch(part):
        rows = pl.ds(part * span, span)
        return pltpu.make_async_copy(boundary_ref.at[rows], boundary.at[rows], sems.at[part])

    fetch_sketch = pltpu.make_async_copy(sketch_ref, sketch, sems.at[parts])
    fetch_sketch.start()
    for part in range(parts):
        fetch(part).start()

    row = lax.broadcasted_iota(jnp.int32, (phys, width), 0)
    col = lax.broadcasted_iota(jnp.int32, (phys, width), 1)
    tiled = jnp.where(lax.rem(col, phys) == row, 1.0, 0.0).astype(jnp.bfloat16)
    repeated = lax.dot_general(
        peps_ref[...], tiled, (((1,), (0,)), ((), ())), preferred_element_type=jnp.float32
    )
    rows = bonds * per
    pick_row = lax.broadcasted_iota(jnp.int32, (rows, bonds), 0)
    pick_col = lax.broadcasted_iota(jnp.int32, (rows, bonds), 1)
    pick = jnp.where(lax.div(pick_row, per) == pick_col, 1.0, 0.0).astype(jnp.bfloat16)
    spread_rows = dot(pick, repeated.astype(jnp.bfloat16))
    out_row = lax.broadcasted_iota(jnp.int32, (rows, width), 0)
    out_col = lax.broadcasted_iota(jnp.int32, (rows, width), 1)
    keep = lax.rem(out_row, per) == lax.div(out_col, phys)
    spread[...] = jnp.where(keep, spread_rows, 0.0).astype(jnp.bfloat16)

    fetch_sketch.wait()
    for lane in range(width // LANES):
        wide[lane] = sketch[:, lane * LANES:(lane + 1) * LANES].astype(jnp.float32)
    for part in range(parts):
        fetch(part).wait()
        for chunk in range(part * chunks, (part + 1) * chunks):
            piece = dot(spread[...], boundary[chunk * width:(chunk + 1) * width, :])
            for bond in range(bonds):
                absorbed[bond, chunk * per:(chunk + 1) * per, :] = piece[bond * per:(bond + 1) * per]

    total[...] = jnp.zeros_like(total)
    for bond in range(bonds):
        high, low = split(absorbed[bond])
        lanes = [wide[lane, pl.ds(bond, width, stride=bonds), :] for lane in range(width // LANES)]
        part = jnp.concatenate(lanes, axis=1).astype(jnp.bfloat16)
        both = dot(jnp.concatenate([high, low], axis=0), part)
        slot = 1 + charge_ref[bond] * sign_ref[0]
        where = pl.ds(pl.multiple_of(slot * width, width), width)
        total[where, :] += both[:width] + both[width:]
    half = total.shape[0] // 2
    top_ref[...] = total[:half]
    bottom_ref[...] = total[half:]


VMEM = pl.BlockSpec(memory_space=pltpu.VMEM)
SMEM = pl.BlockSpec(memory_space=pltpu.SMEM)
HBM = pl.BlockSpec(memory_space=pltpu.HBM)


def transfer(info, boundary, peps_row, sketch, charges):
    width = boundary.shape[3]
    phys, bonds = peps_row.shape[1:]
    parts = 8
    half = jax.ShapeDtypeStruct((CHARGES * width // 2, width), jnp.float32)
    return pl.pallas_call(
        transfer_kernel,
        out_shape=(half, half),
        in_specs=[SMEM] * 2 + [VMEM, HBM, HBM],
        out_specs=(VMEM, VMEM),
        scratch_shapes=[
            pltpu.VMEM((width * phys, width), jnp.bfloat16),
            pltpu.VMEM((width * bonds, width), jnp.bfloat16),
            pltpu.VMEM((bonds * width // phys, width), jnp.bfloat16),
            pltpu.VMEM((bonds, width, width), jnp.float32),
            pltpu.VMEM((width // LANES, width * bonds, LANES), jnp.float32),
            pltpu.VMEM((CHARGES * width, width), jnp.float32),
            pltpu.SemaphoreType.DMA((parts + 1,)),
        ],
        compiler_params=pltpu.CompilerParams(vmem_limit_bytes=LARGE),
        name="transfer",
    )(info[SIGN], charges[0], peps_row[0].T, boundary.reshape(width * phys, width), sketch.reshape(width * bonds, width))


def call(kernel, outs, scalars, arrays, tiles=0, aliases={}, name=None):
    moved = sum(a.size * a.dtype.itemsize for a in arrays)
    rows, width = 128, 256
    shapes = tuple(jax.ShapeDtypeStruct(*out) for out in outs)
    return pl.pallas_call(
        kernel,
        out_shape=shapes,
        in_specs=[SMEM] * len(scalars) + [VMEM] * len(arrays),
        out_specs=(VMEM,) * len(outs),
        input_output_aliases=aliases,
        cost_estimate=pl.CostEstimate(
            flops=6 * tiles * rows * width * width, bytes_accessed=moved, transcendentals=0
        ),
        compiler_params=pltpu.CompilerParams(vmem_limit_bytes=SMALL),
        name=name,
    )(*scalars, *arrays)


def place_kernel(k, who, y_ref, top_ref, bottom_ref, *refs):
    high_ref, low_ref, *odd_refs = refs[-6:] if not who else refs[-2:]
    half = top_ref.shape[0]
    site = lax.rem(y_ref[0] + k, GROUP)
    at = (2 * site + who) * (2 * half)
    for part, ref in enumerate((top_ref, bottom_ref)):
        where = pl.ds(pl.multiple_of(at + part * half, half), half)
        high, low = split(ref[...])
        high_ref[where, :] = high
        low_ref[where, :] = low
        for pair, odd_ref in enumerate(odd_refs[part::2]):
            @pl.when(site == 2 * pair + 1)
            def _():
                odd_ref[...] = ref[...]


def place(info, k, who, top, bottom, placed, odds):
    half, width = top.shape
    out = ((2 * GROUP * 2 * half, width), jnp.bfloat16)
    outs = (out, out) if who else (out, out) + (((half, width), jnp.float32),) * 4
    before = (*placed, *odds) if not who else placed
    aliases = {3 + i: i for i in range(len(before))}
    got = call(
        functools.partial(place_kernel, k, who), outs, (info[Y],), (top, bottom, *before), 0, aliases, "place"
    )
    return got[:2], (odds if who else got[2:])


def tile(ref, index, width):
    return ref[index * width:(index + 1) * width]


def of_site(refs, site, who, slot, width):
    index = (2 * site + who) * CHARGES + slot
    return [tile(ref, index, width) for ref in refs]


def of_pair(refs, who, reach, width):
    return [tile(ref, 5 * who + 2 - reach, width) for ref in refs]


def product(a, b):
    return dot(a[0], b[0]) + dot(a[1], b[0]) + dot(a[0], b[1])


def pair_kernel(pair, inner_ref, top_ref, bottom_ref, high_ref, low_ref, out_ref):
    width = out_ref.shape[1]
    refs = (high_ref, low_ref)
    first = [of_site(refs, 2 * pair, 0, slot, width) for slot in range(CHARGES)]
    own = [of_site(refs, 2 * pair + 1, 0, slot, width) for slot in range(CHARGES)]
    near = [of_site(refs, 2 * pair + 1, 1, slot, width) for slot in range(CHARGES)]
    outer = jnp.concatenate([top_ref[...], bottom_ref[...]], axis=0)
    outer = jnp.where(inner_ref[0] == 1, outer, 0.0)
    far = [split(tile(outer, slot, width)) for slot in range(CHARGES)]
    sums = (
        ((0, far[2]),),
        ((0, far[1]), (1, own[0])),
        ((0, far[0]), (1, own[1]), (2, near[2])),
        ((1, own[2]), (2, near[1])),
        ((2, near[0]),),
    )
    for index, terms in enumerate(sums):
        out_ref[index * width:(index + 1) * width] = sum(product(first[slot], b) for slot, b in terms)


def split_kernel(own_ref, other_ref, high_ref, low_ref):
    size = own_ref.shape[0]
    for who, ref in enumerate((own_ref, other_ref)):
        high, low = split(ref[...])
        high_ref[who * size:(who + 1) * size] = high
        low_ref[who * size:(who + 1) * size] = low


def halves(state):
    width = state.shape[1] // 2
    parts = []
    for who in range(2):
        high, low = split(state[:, who * width:(who + 1) * width])
        parts.append((jnp.concatenate([high, low], axis=0), high))
    return parts


def apply(part, matrix):
    both, high = part
    rows = high.shape[0]
    first = dot(both, matrix[0])
    return first[:rows] + first[rows:] + dot(high, matrix[1])


def leave_site(site, state, refs, out_o, out_i):
    width = state.shape[1] // 2
    mine, other = halves(state)
    out_o[...] = apply(mine, of_site(refs, site, 0, 0, width))
    out_i[...] = apply(other, of_site(refs, site, 1, 0, width))


def stay_site(site, state, refs, out):
    width = state.shape[1] // 2
    mine, other = halves(state)
    at = lambda who, slot: of_site(refs, site, who, slot, width)
    out[:, :width] = apply(mine, at(0, 1)) + apply(other, at(1, 2))
    out[:, width:] = apply(mine, at(0, 2)) + apply(other, at(1, 1))


def leave_pair(state, refs, out_o, out_i):
    width = state.shape[1] // 2
    mine, other = halves(state)
    at = lambda who, reach: of_pair(refs, who, reach, width)
    out_o[:, :width] = apply(mine, at(0, 2))
    out_o[:, width:] = apply(mine, at(0, 1)) + apply(other, at(1, -2))
    out_i[:, :width] = apply(other, at(1, 1)) + apply(mine, at(0, -2))
    out_i[:, width:] = apply(other, at(1, 2))


def stay_pair(state, refs, out):
    width = state.shape[1] // 2
    mine, other = halves(state)
    at = lambda who, reach: of_pair(refs, who, reach, width)
    out[:, :width] = apply(mine, at(0, 0)) + apply(other, at(1, -1))
    out[:, width:] = apply(mine, at(0, -1)) + apply(other, at(1, 0))


def summed_site(inner_ref, past_ref, stay_ref, from_o, from_i):
    own = stay_ref[...]
    width = own.shape[1] // 2
    mine = own[:, :width] + jnp.where(inner_ref[0] == 1, from_i[...], 0.0)
    other = own[:, width:] + jnp.where(past_ref[0] == 1, from_o[...], 0.0)
    return jnp.concatenate([mine, other], axis=1)


def summed_pair(inner_ref, past_ref, stay_ref, from_o, from_i):
    return (
        stay_ref[...]
        + jnp.where(inner_ref[0] == 1, from_i[...], 0.0)
        + jnp.where(past_ref[0] == 1, from_o[...], 0.0)
    )


def leave_site_kernel(site, state_ref, high_ref, low_ref, out_o, out_i):
    leave_site(site, state_ref[...], (high_ref, low_ref), out_o, out_i)


def stay_site_kernel(site, state_ref, high_ref, low_ref, out):
    stay_site(site, state_ref[...], (high_ref, low_ref), out)


def next_site_kernel(site, summing, inner_ref, past_ref, stay_ref, from_o, from_i, high_ref, low_ref, state_ref, out_o, out_i):
    state = summing(inner_ref, past_ref, stay_ref, from_o, from_i)
    state_ref[...] = state
    leave_site(site, state, (high_ref, low_ref), out_o, out_i)


def last_kernel(summing, inner_ref, past_ref, stay_ref, from_o, from_i, state_ref):
    state_ref[...] = summing(inner_ref, past_ref, stay_ref, from_o, from_i)


def leave_pair_kernel(state_ref, high_ref, low_ref, out_o, out_i):
    leave_pair(state_ref[...], (high_ref, low_ref), out_o, out_i)


def stay_pair_kernel(state_ref, high_ref, low_ref, out):
    stay_pair(state_ref[...], (high_ref, low_ref), out)


def next_pair_kernel(inner_ref, past_ref, stay_ref, from_o, from_i, high_ref, low_ref, state_ref, out_o, out_i):
    state = summed_pair(inner_ref, past_ref, stay_ref, from_o, from_i)
    state_ref[...] = state
    leave_pair(state, (high_ref, low_ref), out_o, out_i)


def half_kernel(starts_ref, high_ref, low_ref, out, out_o, out_i):
    rows = starts_ref.shape[1]
    refs = (high_ref, low_ref)
    for pair in range(GROUP // 2):
        where = pl.ds(pair * rows, rows)
        state = starts_ref[pair]
        stay_site(2 * pair, state, refs, out.at[pair])
        leave_site(2 * pair, state, refs, out_o.at[where], out_i.at[where])


def half_sum_kernel(inner_ref, past_ref, stay_ref, from_o, from_i, old_ref, kept_ref):
    rows = stay_ref.shape[1]
    for pair in range(GROUP // 2):
        where = pl.ds(pair * rows, rows)
        kept_ref[2 * pair] = summed_site(inner_ref, past_ref, stay_ref.at[pair], from_o.at[where], from_i.at[where])


def keep_kernel(phase, site, x_ref, state_ref, *refs):
    @pl.when(x_ref[0] == phase)
    def _():
        refs[-1][site] = state_ref[...]


def edge_kernel(y_ref, core_ref, edge_ref, mine_ref, other_ref):
    rows = mine_ref.shape[0]
    for ref, core in ((mine_ref, core_ref[0]), (other_ref, 1 - core_ref[0])):
        at = pl.multiple_of((2 * y_ref[0] + core) * rows, rows)
        ref[...] = edge_ref[pl.ds(at, rows), :].astype(jnp.float32)


def give_kernel(kept_ref, out_ref):
    width = out_ref.shape[2]
    out_ref[...] = kept_ref[:, :, width:]


def slab_of(kept_ref, given_ref, core, site):
    width = given_ref.shape[2]
    mine, given = kept_ref[site, :, :width], given_ref[site]
    return jnp.concatenate([jnp.where(core == 0, mine, given), jnp.where(core == 0, given, mine)], axis=0)


def pick_kernel(y_ref, core_ref, kept_ref, given_ref, *outs):
    for by, out in enumerate(outs):
        out[...] = slab_of(kept_ref, given_ref, core_ref[0], lax.rem(y_ref[0] + by + 1, GROUP))


def lay_kernel(y_ref, core_ref, kept_ref, given_ref, *refs):
    out_ref = refs[-1]
    slab = 2 * kept_ref.shape[1]
    for by in range(GROUP):
        source = lax.rem(y_ref[0] + GROUP - by, GROUP)
        where = pl.ds(pl.multiple_of(source * slab, slab), slab)
        out_ref[0, where, :] = refs[by - 1][...] if by else slab_of(kept_ref, given_ref, core_ref[0], y_ref[0])


X, Y, SIGN, INNER, PAST, CORE = range(6)


def local(boundary, peps_row, sketch, charges, left_edge):
    sites = lax.axis_size("site")
    sectors = lax.axis_size("sector")
    position = lax.axis_index("site")
    block = lax.axis_index("sector")
    rows, width = left_edge.shape
    slab = rows // GROUP
    part = slab // 2
    single = ((part, width), jnp.float32)
    double = ((part, 2 * width), jnp.float32)
    kept_shape = ((GROUP, part, 2 * width), jnp.float32)
    starts_shape = ((GROUP // 2, part, 2 * width), jnp.float32)

    inside = [(i, i ^ 1) for i in range(sectors)]
    across = [(i, (i - 1) % sectors if i % 2 == 0 else (i + 1) % sectors) for i in range(sectors)]
    outward = [(i, (i - 2) % sectors if i % 2 == 0 else (i + 2) % sectors) for i in range(sectors)]
    inward = [(i, (i + 2) % sectors if i % 2 == 0 else (i - 2) % sectors) for i in range(sectors)]
    ring = lambda by: [(i, i - i % GROUP + (i + by) % GROUP) for i in range(sites)]
    hop = [(i, (i + GROUP) % sites) for i in range(sites)]
    over_sector = lambda array, pairs: lax.ppermute(array, "sector", pairs)

    core = lax.rem(block, 2)
    inner = jnp.logical_and(block > 0, block < sectors - 1)
    past = jnp.logical_and(block != 1, block != sectors - 2)
    info = [lax.div(position, GROUP), lax.rem(position, GROUP), 1 - 2 * core, inner, past, core]
    info = lax.optimization_barrier([scalar.astype(jnp.int32).reshape(1) for scalar in info])
    limits = (info[INNER], info[PAST])

    top, bottom = transfer(info, boundary, peps_row, sketch, charges)
    up_top = lax.ppermute(top, "site", ring(-1))
    down_bottom = lax.ppermute(bottom, "site", ring(1))
    up_bottom = lax.ppermute(bottom, "site", ring(-1))
    down_top = lax.ppermute(top, "site", ring(1))
    mine, give = call(edge_kernel, (single,) * 2, (info[Y], info[CORE]), (left_edge,), name="edge")
    state = jnp.concatenate([mine, over_sector(give, inside)], axis=1)
    placed, odds = (), ()

    def settle(k, pieces, placed, odds):
        placed, odds = place(info, k, 0, *pieces, placed, odds)
        others = [over_sector(piece, inside) for piece in pieces]
        return place(info, k, 1, *others, placed, odds)

    placed, odds = settle(0, (top, bottom), placed, odds)
    placed, odds, state, up_top, down_bottom = lax.optimization_barrier((placed, odds, state, up_top, down_bottom))
    far_top = lax.ppermute(up_top, "site", ring(-1))
    far_bottom = lax.ppermute(down_bottom, "site", ring(1))
    placed, odds = settle(1, (up_top, up_bottom), placed, odds)
    placed, odds = settle(3, (down_top, down_bottom), placed, odds)
    placed, odds = settle(2, (far_top, far_bottom), placed, odds)

    kept = starts = None

    def keep(phase, slot, value, into, shape):
        arrays = (value,) if into is None else (value, into)
        aliases = {} if into is None else {2: 0}
        return call(functools.partial(keep_kernel, phase, slot), (shape,), (info[X],), arrays, 0, aliases, "keep")[0]

    out_o, out_i = call(
        functools.partial(leave_site_kernel, 0), (single,) * 2, (), (state, *placed), 1, name="leave_site"
    )
    outers, matrices = [], []

    def matrix(pair):
        product_shape = ((5 * width, width), jnp.float32)
        arrays = (*outers[2 * pair:2 * pair + 2], *placed)
        own, = call(functools.partial(pair_kernel, pair), (product_shape,), (info[INNER],), arrays, 18, name="pair")
        arrays = (own, over_sector(own, inside))
        matrices.append(call(split_kernel, (((10 * width, width), jnp.bfloat16),) * 2, (), arrays, name="split"))

    for site in range(GROUP):
        if site % 2 == 0:
            starts = keep(0, site // 2, state, starts, starts_shape)
        from_o, from_i = over_sector(out_o, outward), over_sector(out_i, inward)
        stay, = call(functools.partial(stay_site_kernel, site), (double,), (), (state, *placed), WINDOW, name="stay_site")
        stay, odd = lax.optimization_barrier((stay, odds[site]))
        outers.append(over_sector(odd, across))
        if site == GROUP - 1:
            stay, outers[:2] = lax.optimization_barrier((stay, outers[:2]))
            matrix(0)
        arrays = (stay, from_o, from_i)
        if site < GROUP - 1:
            state, out_o, out_i = call(
                functools.partial(next_site_kernel, site + 1, summed_site), (double, single, single), limits, (*arrays, *placed), 1,
                name="next_site",
            )
        else:
            state, = call(functools.partial(last_kernel, summed_site), (double,), limits, arrays, name="last")
        if site % 2:
            kept = keep(0, site, state, kept, kept_shape)

    for phase in range(1, sites // GROUP):
        state = lax.ppermute(state, "site", hop)
        out_o, out_i = call(leave_pair_kernel, (double,) * 2, (), (state, *matrices[0]), 3, name="leave_pair")
        for pair in range(GROUP // 2):
            starts = keep(phase, pair, state, starts, starts_shape)
            alone = phase == 1 and pair == 1
            for site in range(2 * pair, 2 * pair + 2) if alone else (2 * pair + 1,):
                from_o, from_i = over_sector(out_o, outward), over_sector(out_i, inward)
                if alone:
                    kernel, arrays = functools.partial(stay_site_kernel, site), (state, *placed)
                else:
                    kernel, arrays = stay_pair_kernel, (state, *matrices[pair])
                stay, = call(kernel, (double,), (), arrays, WINDOW, name="stay")
                if alone and site == 2 * pair:
                    stay, outers[2:] = lax.optimization_barrier((stay, outers[2:]))
                    matrix(1)
                summing = summed_site if alone else summed_pair
                arrays = (stay, from_o, from_i)
                if site == GROUP - 1:
                    state, = call(functools.partial(last_kernel, summing), (double,), limits, arrays, name="last")
                elif phase == 1:
                    kernel = functools.partial(next_site_kernel, site + 1, summing)
                    state, out_o, out_i = call(
                        kernel, (double, single, single), limits, (*arrays, *placed), 1, name="next_site"
                    )
                else:
                    state, out_o, out_i = call(
                        next_pair_kernel, (double,) * 3, limits, (*arrays, *matrices[pair + 1]), 3, name="next_pair"
                    )
            kept = keep(phase, 2 * pair + 1, state, kept, kept_shape)

    stacked = ((slab, width), jnp.float32)
    half, half_o, half_i = call(half_kernel, (starts_shape, stacked, stacked), (), (starts, *placed), 6, name="half")
    half_o, half_i = over_sector(half_o, outward), over_sector(half_i, inward)
    kept, = call(half_sum_kernel, (kept_shape,), limits, (half, half_o, half_i, kept), 0, {5: 0}, "half_sum")

    given_shape = ((GROUP, part, width), jnp.float32)
    given, = call(give_kernel, (given_shape,), (), (kept,), name="give")
    given = over_sector(given, inside)
    where = (info[Y], info[CORE])
    sent = call(pick_kernel, (((slab, width), jnp.float32),) * (GROUP - 1), where, (kept, given), name="pick")
    came = [lax.ppermute(out, "site", ring(by + 1)) for by, out in enumerate(sent)]
    result, = call(lay_kernel, (((1, rows, width), jnp.float32),), where, (kept, given, *came), name="lay")
    return result


def solution(mesh):
    in_specs = (
        P("site", "sector", None, None),
        P("site", None, None),
        P("site", "sector", None, None),
        P("site", None),
        P(None, "sector"),
    )
    out_specs = P("site", None, "sector")
    return jax.shard_map(local, mesh=mesh, in_specs=in_specs, out_specs=out_specs, check_vma=False)
```

```python
import functools

import jax
import jax.numpy as jnp
from jax import lax
from jax.experimental import pallas as pl
from jax.experimental.pallas import tpu as pltpu
from jax.sharding import PartitionSpec as P

GROUP = 4
CHARGES = 3
LANES = 128
SMALL = 12 * 2**20
LARGE = 56 * 2**20


def dot(a, b):
    return jnp.dot(a, b, preferred_element_type=jnp.float32)


def split(x):
    high = x.astype(jnp.bfloat16)
    return high, (x - high.astype(jnp.float32)).astype(jnp.bfloat16)


def transfer_kernel(x_ref, y_ref, sign_ref, inner_ref, charge_ref, peps_ref, boundary_ref, sketch_ref, top_ref, bottom_ref,
                    boundary, sketch, spread, absorbed, wide, total, sems):
    width = total.shape[1]
    bonds, phys = peps_ref.shape
    per = width // phys
    parts = sems.shape[0] - 1
    span = boundary.shape[0] // parts
    chunks = span // width

    def fetch(part):
        rows = pl.ds(part * span, span)
        return pltpu.make_async_copy(boundary_ref.at[rows], boundary.at[rows], sems.at[part])

    fetch_sketch = pltpu.make_async_copy(sketch_ref, sketch, sems.at[parts])
    for part in range(parts):
        fetch(part).start()
    fetch_sketch.start()

    row = lax.broadcasted_iota(jnp.int32, (phys, width), 0)
    col = lax.broadcasted_iota(jnp.int32, (phys, width), 1)
    tiled = jnp.where(lax.rem(col, phys) == row, 1.0, 0.0).astype(jnp.bfloat16)
    repeated = lax.dot_general(
        peps_ref[...], tiled, (((1,), (0,)), ((), ())), preferred_element_type=jnp.float32
    )
    rows = bonds * per
    pick_row = lax.broadcasted_iota(jnp.int32, (rows, bonds), 0)
    pick_col = lax.broadcasted_iota(jnp.int32, (rows, bonds), 1)
    pick = jnp.where(lax.div(pick_row, per) == pick_col, 1.0, 0.0).astype(jnp.bfloat16)
    spread_rows = dot(pick, repeated.astype(jnp.bfloat16))
    out_row = lax.broadcasted_iota(jnp.int32, (rows, width), 0)
    out_col = lax.broadcasted_iota(jnp.int32, (rows, width), 1)
    keep = lax.rem(out_row, per) == lax.div(out_col, phys)
    spread[...] = jnp.where(keep, spread_rows, 0.0).astype(jnp.bfloat16)

    for part in range(parts):
        fetch(part).wait()
        for chunk in range(part * chunks, (part + 1) * chunks):
            piece = dot(spread[...], boundary[chunk * width:(chunk + 1) * width, :])
            for bond in range(bonds):
                absorbed[bond, chunk * per:(chunk + 1) * per, :] = piece[bond * per:(bond + 1) * per]

    fetch_sketch.wait()
    for lane in range(width // LANES):
        wide[lane] = sketch[:, lane * LANES:(lane + 1) * LANES].astype(jnp.float32)
    total[...] = jnp.zeros_like(total)
    for bond in range(bonds):
        high, low = split(absorbed[bond])
        lanes = [wide[lane, pl.ds(bond, width, stride=bonds), :] for lane in range(width // LANES)]
        part = jnp.concatenate(lanes, axis=1).astype(jnp.bfloat16)
        both = dot(jnp.concatenate([high, low], axis=0), part)
        slot = 1 + charge_ref[bond] * sign_ref[0]
        where = pl.ds(pl.multiple_of(slot * width, width), width)
        total[where, :] += both[:width] + both[width:]
    half = total.shape[0] // 2
    top_ref[...] = total[:half]
    bottom_ref[...] = total[half:]


VMEM = pl.BlockSpec(memory_space=pltpu.VMEM)
SMEM = pl.BlockSpec(memory_space=pltpu.SMEM)
ANY = pl.BlockSpec(memory_space=pl.ANY)


def transfer(info, boundary, peps_row, sketch, charges):
    width = boundary.shape[3]
    phys, bonds = peps_row.shape[1:]
    parts = 8
    half = jax.ShapeDtypeStruct((CHARGES * width // 2, width), jnp.float32)
    return pl.pallas_call(
        transfer_kernel,
        out_shape=(half, half),
        in_specs=[SMEM] * 5 + [VMEM, ANY, ANY],
        out_specs=(VMEM, VMEM),
        scratch_shapes=[
            pltpu.VMEM((width * phys, width), jnp.bfloat16),
            pltpu.VMEM((width * bonds, width), jnp.bfloat16),
            pltpu.VMEM((bonds * width // phys, width), jnp.bfloat16),
            pltpu.VMEM((bonds, width, width), jnp.float32),
            pltpu.VMEM((width // LANES, width * bonds, LANES), jnp.float32),
            pltpu.VMEM((CHARGES * width, width), jnp.float32),
            pltpu.SemaphoreType.DMA((parts + 1,)),
        ],
        compiler_params=pltpu.CompilerParams(vmem_limit_bytes=LARGE),
        name="transfer",
    )(*info, charges[0], peps_row[0].T, boundary.reshape(width * phys, width), sketch.reshape(width * bonds, width))


def times(state, high, low):
    rows = state.shape[0]
    state_high, state_low = split(state)
    first = dot(jnp.concatenate([state_high, state_low], axis=0), high)
    return first[:rows] + first[rows:] + dot(state_high, low)


def call(kernel, outs, scalars, arrays, tiles=0, aliases={}, name=None):
    moved = sum(a.size * a.dtype.itemsize for a in arrays)
    rows, width = 128, 256
    shapes = tuple(jax.ShapeDtypeStruct(*out) for out in outs)
    return pl.pallas_call(
        kernel,
        out_shape=shapes,
        in_specs=[SMEM] * len(scalars) + [VMEM] * len(arrays),
        out_specs=(VMEM,) * len(outs),
        input_output_aliases=aliases,
        cost_estimate=pl.CostEstimate(
            flops=6 * tiles * rows * width * width, bytes_accessed=moved, transcendentals=0
        ),
        compiler_params=pltpu.CompilerParams(vmem_limit_bytes=SMALL),
        name=name,
    )(*scalars, *arrays)


def place_kernel(k, y_ref, top_ref, bottom_ref, *refs):
    high_ref, low_ref = refs[-2:]
    half = top_ref.shape[0]
    at = lax.rem(y_ref[0] + k, GROUP) * (2 * half)
    for ref, offset in ((top_ref, 0), (bottom_ref, half)):
        where = pl.ds(pl.multiple_of(at + offset, half), half)
        high, low = split(ref[...])
        high_ref[where, :] = high
        low_ref[where, :] = low


def place(info, k, top, bottom, placed):
    half, width = top.shape
    out = ((GROUP * 2 * half, width), jnp.bfloat16)
    aliases = {3: 0, 4: 1} if placed else {}
    return call(
        functools.partial(place_kernel, k), (out, out), (info[Y],), (top, bottom, *placed), 0, aliases, "place"
    )


def columns(site, slot, width):
    start = (site * CHARGES + slot) * width
    return slice(start, start + width)


def away_of(site, state, high_ref, low_ref, out_a, out_b):
    width = state.shape[1]
    for slot, out in ((0, out_b), (2, out_a)):
        where = columns(site, slot, width)
        out[...] = times(state, high_ref[where], low_ref[where])


def edge_kernel(y_ref, edge_ref, state_ref):
    slab = state_ref.shape[0]
    at = pl.multiple_of(y_ref[0] * slab, slab)
    state_ref[...] = edge_ref[pl.ds(at, slab), :].astype(jnp.float32)


def away_kernel(state_ref, high_ref, low_ref, out_a, out_b):
    away_of(0, state_ref[...], high_ref, low_ref, out_a, out_b)


def summed(inner_ref, stay_ref, from_a, from_b):
    return stay_ref[...] + from_a[...] + jnp.where(inner_ref[0] == 1, from_b[...], 0.0)


def sum_away_kernel(site, inner_ref, stay_ref, from_a, from_b, high_ref, low_ref, state_ref, out_a, out_b):
    state = summed(inner_ref, stay_ref, from_a, from_b)
    state_ref[...] = state
    away_of(site, state, high_ref, low_ref, out_a, out_b)


def keep_at(phase, site, x_ref, state, kept_ref):
    @pl.when(x_ref[0] == phase)
    def _():
        kept_ref[site] = state


def stay_kernel(phase, site, x_ref, state_ref, high_ref, low_ref, *refs):
    where = columns(site, 1, state_ref.shape[1])
    state = state_ref[...]
    if site:
        keep_at(phase, site - 1, x_ref, state, refs[-1])
        out_ref = refs[-2]
    else:
        out_ref = refs[-1]
    out_ref[...] = times(state, high_ref[where], low_ref[where])


def sum_kernel(inner_ref, stay_ref, from_a, from_b, state_ref):
    state_ref[...] = summed(inner_ref, stay_ref, from_a, from_b)


def keep_kernel(phase, x_ref, state_ref, old_ref, kept_ref):
    keep_at(phase, GROUP - 1, x_ref, state_ref[...], kept_ref)


def pick_kernel(y_ref, kept_ref, *outs):
    for by, out in enumerate(outs):
        out[...] = kept_ref[lax.rem(y_ref[0] + by + 1, GROUP)]


def lay_kernel(y_ref, kept_ref, *refs):
    out_ref = refs[-1]
    slab = kept_ref.shape[1]
    for by in range(GROUP):
        source = lax.rem(y_ref[0] + GROUP - by, GROUP)
        where = pl.ds(pl.multiple_of(source * slab, slab), slab)
        out_ref[0, where, :] = refs[by - 1][...] if by else kept_ref[y_ref[0]]


X, Y, SIGN, INNER = range(4)


def local(boundary, peps_row, sketch, charges, left_edge):
    sites = lax.axis_size("site")
    sectors = lax.axis_size("sector")
    position = lax.axis_index("site")
    block = lax.axis_index("sector")
    rows, width = left_edge.shape
    slab = rows // GROUP
    state_shape = ((slab, width), jnp.float32)
    kept_shape = ((GROUP, slab, width), jnp.float32)

    inside = [(i, i ^ 1) for i in range(sectors)]
    across = [(i, (i - 1) % sectors if i % 2 == 0 else (i + 1) % sectors) for i in range(sectors)]
    ring = lambda by: [(i, i - i % GROUP + (i + by) % GROUP) for i in range(sites)]
    hop = [(i, (i + GROUP) % sites) for i in range(sites)]

    inner = jnp.logical_and(block > 0, block < sectors - 1).astype(jnp.int32)
    info = [lax.div(position, GROUP), lax.rem(position, GROUP), 1 - 2 * lax.rem(block, 2), inner]
    info = lax.optimization_barrier([scalar.astype(jnp.int32).reshape(1) for scalar in info])

    top, bottom = transfer(info, boundary, peps_row, sketch, charges)
    up_top = lax.ppermute(top, "site", ring(-1))
    down_bottom = lax.ppermute(bottom, "site", ring(1))
    up_bottom = lax.ppermute(bottom, "site", ring(-1))
    down_top = lax.ppermute(top, "site", ring(1))
    state, = call(edge_kernel, (state_shape,), (info[Y],), (left_edge,), name="edge")
    placed = place(info, 0, top, bottom, ())
    placed, state, up_top, down_bottom = lax.optimization_barrier((placed, state, up_top, down_bottom))
    far_top = lax.ppermute(up_top, "site", ring(-1))
    far_bottom = lax.ppermute(down_bottom, "site", ring(1))
    placed = place(info, 1, up_top, up_bottom, placed)
    placed = place(info, 3, down_top, down_bottom, placed)
    placed = place(info, 2, far_top, far_bottom, placed)

    kept = None
    for phase in range(sites // GROUP):
        if phase:
            state = lax.ppermute(state, "site", hop)
        out_a, out_b = call(away_kernel, (state_shape,) * 2, (), (state, *placed), 2, name="away")
        for site in range(GROUP):
            from_b = lax.ppermute(out_b, "sector", across)
            from_a = lax.ppermute(out_a, "sector", inside)
            kernel = functools.partial(stay_kernel, phase, site)
            arrays = (state, *placed)
            if not site:
                stay, = call(kernel, (state_shape,), (info[X],), arrays, 1, name="stay")
            elif kept is None:
                stay, kept = call(kernel, (state_shape, kept_shape), (info[X],), arrays, 1, name="stay")
            else:
                stay, kept = call(kernel, (state_shape, kept_shape), (info[X],), (*arrays, kept), 1, {4: 1}, "stay")
            if site < GROUP - 1:
                kernel = functools.partial(sum_away_kernel, site + 1)
                arrays = (stay, from_a, from_b, *placed)
                state, out_a, out_b = call(kernel, (state_shape,) * 3, (info[INNER],), arrays, 2, name="sum_away")
            else:
                state, = call(sum_kernel, (state_shape,), (info[INNER],), (stay, from_a, from_b), name="sum")
                kernel = functools.partial(keep_kernel, phase)
                kept, = call(kernel, (kept_shape,), (info[X],), (state, kept), 0, {2: 0}, "keep")

    sent = call(pick_kernel, (state_shape,) * (GROUP - 1), (info[Y],), (kept,), name="pick")
    came = [lax.ppermute(out, "site", ring(by + 1)) for by, out in enumerate(sent)]
    result, = call(lay_kernel, (((1, rows, width), jnp.float32),), (info[Y],), (kept, *came), name="lay")
    return result


def solution(mesh):
    in_specs = (
        P("site", "sector", None, None),
        P("site", None, None),
        P("site", "sector", None, None),
        P("site", None),
        P(None, "sector"),
    )
    out_specs = P("site", None, "sector")
    return jax.shard_map(local, mesh=mesh, in_specs=in_specs, out_specs=out_specs, check_vma=False)
```
